32 devices in a mesh: seg: 8 (over z, x), grp: 4 (over y, core).
Axes of the slice: x: 2, y: 2, z: 4, core: 2. Of those that a mesh axis runs over, the one named last changes fastest.
Arguments:
- snapshots: float32 [49152, 512], P(('seg', 'grp')), as said below
- upstream: int32 [49152], P(('seg', 'grp')), may hold values from -1 to 49150, as said below
- velocity: float32 [49152], P(('seg', 'grp')), may hold values from 0.5 to 4
Outputs:
- reduced_operator: float32 [512, 512], replicated
- triangle: float32 [512, 512], replicated
The draws below stay inside these ranges and needn't reach their ends.
Inputs may be any that keep to these rules, and one draw needn't show every extreme that they name: Segment g = p * 1536 + l lies in partition p. For l >= 512 its upstream is a segment of the same partition with a smaller index, and for l = 1535 it is g - 1. For l < 512 its upstream lies in the last 512 segments of partition p - 1, and the first segment of each partition p >= 1 takes exactly segment p * 1536 - 512; in partition 0 these segments have upstream -1, and no other segment has. `snapshots`: Real-valued fields of full rank.
All inputs are finite; a program needn't handle non-finite values.
Results may differ from the reference program's by a relative error of at most 0.0003.
Values sent between devices are 32-bit elements; how exact they have to be, the bound alone decides.
A program may use at most 128 MiB of HBM per device.

```python
import math
import jax
import jax.numpy as jnp
from jax import lax

K = 512
ROWS_DEV = 1536
EDGE = 512
INLETS = 512
ROWS = 49152


def upstream_table(key):
    base = jax.random.fold_in(key, 11)
    rows_all = jnp.arange(ROWS, dtype=jnp.int32)
    block = rows_all // ROWS_DEV
    place = rows_all % ROWS_DEV
    picks = jax.random.randint(jax.random.fold_in(base, 1), (ROWS,), 0, EDGE)
    picks = jnp.where(place == 0, 0, picks)
    inlet = jnp.where(block == 0, -1, block * ROWS_DEV - EDGE + picks)
    inner = block * ROWS_DEV + jax.random.randint(jax.random.fold_in(base, 2), (ROWS,), 0, jnp.maximum(place, 1))
    inner = jnp.where(place == ROWS_DEV - 1, rows_all - 1, inner)
    return jnp.where(place < INLETS, inlet, inner).astype(jnp.int32)


def draw_upstream(key, part):
    return upstream_table(key)


def draw_snapshots(key, part):
    feeds = upstream_table(key)
    base = jax.random.fold_in(key, 23)
    noise = jax.random.normal(jax.random.fold_in(base, 1), (ROWS, K), jnp.float32)
    colscale = jnp.exp(jax.random.uniform(jax.random.fold_in(base, 2), (K,), jnp.float32, 0.0, math.log(10.0)))
    carried = jax.random.uniform(jax.random.fold_in(base, 4), (K,), jnp.float32, 0.1, 0.95)
    kept = jnp.sqrt(1.0 - carried * carried)
    earlier = jnp.take(noise, jnp.maximum(feeds, 0), axis=0)
    mixed = jnp.where(feeds[:, None] >= 0, kept[None, :] * noise + carried[None, :] * earlier, noise)
    shaped = mixed
    weights = (0.3, 0.25, 0.2)
    for index in range(3):
        order = jax.random.permutation(jax.random.fold_in(base, 10 + index), K)
        shaped = shaped + weights[index] * jnp.take(mixed, order, axis=1)
    return (shaped * colscale[None, :]).astype(jnp.float32)


def block_levels(rng, shape, cuts, least, top_value):
    def one(dim, shards_of):
        heights = jax.random.uniform(jax.random.fold_in(jax.random.fold_in(rng, 6), dim), (shards_of,), jnp.float32, least / len(cuts), top_value / len(cuts))
        return jnp.repeat(jnp.exp(heights), shape[dim] // shards_of).reshape((-1,) + (1,) * (len(shape) - dim - 1))

    factor_of = one(*cuts[0])
    for cut in cuts[1:]:
        factor_of = factor_of * one(*cut)
    return factor_of


def setup_inputs(seed: int = 0) -> dict:
    key_list = jax.random.split(jax.random.key(seed), 4)
    snapshots = draw_snapshots(jax.random.fold_in(key_list[3], 71), 0)
    upstream = draw_upstream(jax.random.fold_in(key_list[3], 71), 0)
    velocity = jnp.clip(jnp.exp(math.log(4.0) - 2.0794415 * jax.random.uniform(key_list[2], (ROWS,), jnp.float32) ** block_levels(key_list[2], (ROWS,), ((0, 32),), -0.2, 0.2)), 0.5, 4.0)
    return {"snapshots": snapshots, "upstream": upstream, "velocity": velocity}


def reference(snapshots, upstream, velocity):
    high = lax.Precision.HIGHEST
    blocks = ROWS // ROWS_DEV
    width = snapshots.shape[1]
    xs = snapshots.reshape(blocks, ROWS_DEV, width)
    ups = upstream.reshape(blocks, ROWS_DEV)
    vel = velocity.reshape(blocks, ROWS_DEV)

    def add_gram(total, block):
        return (total + jnp.dot(block.T.astype(jnp.float32), block.astype(jnp.float32), precision=high, preferred_element_type=jnp.float32), None)
    gram, _ = lax.scan(add_gram, jnp.zeros((width, width), jnp.float32), xs)
    gram = gram / ROWS
    lower = jnp.linalg.cholesky(gram)
    scale = 1.0 / math.sqrt(ROWS)

    def add_block(carry, item):
        total, previous = carry
        block, ups_b, vel_b, index = item
        basis = jax.scipy.linalg.solve_triangular(lower, block.T, lower=True).T * scale
        extended = jnp.concatenate([previous, basis], 0)
        position = (ups_b - (index * ROWS_DEV - EDGE)).astype(jnp.int32)
        image = vel_b[:, None] * (jnp.take(extended, position, axis=0) - basis)
        total = total + jnp.dot(basis.T.astype(jnp.float32), image.astype(jnp.float32), precision=high, preferred_element_type=jnp.float32)
        return ((total, basis[ROWS_DEV - EDGE:]), None)
    start = (jnp.zeros((width, width), jnp.float32), jnp.zeros((EDGE, width), jnp.float32))
    (operator, _), _ = lax.scan(add_block, start, (xs, ups, vel, jnp.arange(blocks, dtype=jnp.int32)))
    return (operator, lower.T)
```

```python
import jax
import jax.numpy as jnp
from jax import lax
from jax.experimental import pallas as pl
from jax.experimental.pallas import tpu as pltpu
from jax.sharding import PartitionSpec as P

EDGE = 512
NB = 64
GROUP = 4
AXES = ("seg", "grp")


def dot32(a, b, dims):
    return lax.dot_general(
        a,
        b,
        (dims, ((), ())),
        precision=lax.Precision.HIGHEST,
        preferred_element_type=jnp.float32,
    )


def eliminate(block):
    rows = lax.broadcasted_iota(jnp.int32, (NB, 2 * NB), 0)
    lanes = lax.broadcasted_iota(jnp.int32, (NB, 2 * NB), 1)
    unit = (rows + NB == lanes).astype(jnp.float32)
    work = jnp.concatenate([block, unit[:, NB:]], 1)
    for k in range(0, NB, GROUP):
        cols = [
            jnp.broadcast_to(work[:, k + i : k + i + 1], (NB, 2 * NB))
            for i in range(GROUP)
        ]
        lines = [work[k + i : k + i + 1, :] for i in range(GROUP)]
        piv = [[cols[j][k + i : k + i + 1, :] for j in range(GROUP)] for i in range(GROUP)]
        for i in range(GROUP):
            inv = 1.0 / piv[i][i]
            scaled = lines[i] * inv
            below = jnp.where(rows > k + i, cols[i], 0.0)
            work = work - below * scaled
            for j in range(i + 1, GROUP):
                f = piv[j][i] * inv
                lines[j] = lines[j] - f * lines[i]
                g = piv[i][j] * inv
                cols[j] = cols[j] - below * g
                for m in range(i + 1, GROUP):
                    piv[j][m] = piv[j][m] - f * piv[i][m]
    diag = jnp.sum(jnp.where(rows == lanes, work, 0.0), axis=1, keepdims=True)
    work = work * lax.rsqrt(diag)
    keep = (lanes >= rows) & ((lanes < NB) | (lanes <= rows + NB))
    return jnp.where(keep, work, 0.0)


def factor_kernel(gram_ref, upper_ref, inverse_ref, a_ref):
    order = gram_ref.shape[0]
    a_ref[...] = gram_ref[...]
    upper_ref[...] = jnp.zeros_like(upper_ref)
    r = lax.broadcasted_iota(jnp.int32, (order, order), 0)
    c = lax.broadcasted_iota(jnp.int32, (order, order), 1)
    inverse_ref[...] = (r == c).astype(jnp.float32)
    for lo in range(0, order, NB):
        hi = lo + NB
        done = eliminate(a_ref[lo:hi, lo:hi])
        inv = done[:, NB:]
        upper_ref[lo:hi, lo:hi] = done[:, :NB]
        new = dot32(inv, inverse_ref[lo:hi, :], ((1,), (0,)))
        inverse_ref[lo:hi, :] = new
        if hi < order:
            line = dot32(inv, a_ref[lo:hi, hi:], ((1,), (0,)))
            upper_ref[lo:hi, hi:] = line
            a_ref[hi:, hi:] = a_ref[hi:, hi:] - dot32(line, line, ((0,), (0,)))
            inverse_ref[hi:, :] = inverse_ref[hi:, :] - dot32(line, new, ((0,), (0,)))


def factor(gram):
    order = gram.shape[0]
    shape = jax.ShapeDtypeStruct((order, order), jnp.float32)
    return pl.pallas_call(
        factor_kernel,
        out_shape=(shape, shape),
        in_specs=[pl.BlockSpec(memory_space=pltpu.VMEM)],
        out_specs=(pl.BlockSpec(memory_space=pltpu.VMEM),) * 2,
        scratch_shapes=[pltpu.VMEM((order, order), jnp.float32)],
        compiler_params=pltpu.CompilerParams(vmem_limit_bytes=32 * 1024 * 1024),
        cost_estimate=pl.CostEstimate(
            flops=12 * order**3, bytes_accessed=12 * order**2, transcendentals=0
        ),
    )(gram)


def from_behind(block):
    count = lax.axis_size(AXES)
    route = [(i - 1, i) for i in range(1, count)]
    return lax.ppermute(block, AXES, route)


def shards(snapshots, upstream, velocity):
    high = lax.Precision.HIGH
    rows_here = snapshots.shape[0]
    count = rows_here * lax.axis_size(AXES)
    first_row = lax.axis_index(AXES) * rows_here
    arrived = from_behind(snapshots[rows_here - EDGE :])
    local_gram = jnp.dot(
        snapshots.T, snapshots, precision=high, preferred_element_type=jnp.float32
    )
    gram = lax.psum(local_gram, AXES) / count
    extended = jnp.concatenate([arrived, snapshots], 0)
    position = upstream - (first_row - EDGE)
    image = velocity[:, None] * (jnp.take(extended, position, axis=0) - snapshots)
    local_term = jnp.dot(
        snapshots.T, image, precision=high, preferred_element_type=jnp.float32
    )
    term = lax.psum(local_term, AXES) / count
    upper, inverse = factor(gram)
    operator = dot32(dot32(inverse, term, ((1,), (0,))), inverse, ((1,), (1,)))
    return (operator, upper)


def solution(mesh):
    return jax.shard_map(
        shards,
        mesh=mesh,
        in_specs=(P(AXES, None), P(AXES), P(AXES)),
        out_specs=(P(), P()),
        check_vma=False,
    )
```

```python
import functools

import jax
import jax.numpy as jnp
from jax import lax
from jax.experimental import pallas as pl
from jax.experimental.pallas import tpu as pltpu
from jax.sharding import PartitionSpec as P

EDGE = 512
NB = 64
GROUP = 4
AXES = ("seg", "grp")


def dot32(a, b, dims):
    return lax.dot_general(
        a,
        b,
        (dims, ((), ())),
        precision=lax.Precision.HIGHEST,
        preferred_element_type=jnp.float32,
    )


def eliminate(block):
    rows = lax.broadcasted_iota(jnp.int32, (NB, 2 * NB), 0)
    lanes = lax.broadcasted_iota(jnp.int32, (NB, 2 * NB), 1)
    unit = (rows + NB == lanes).astype(jnp.float32)
    work = jnp.concatenate([block, unit[:, NB:]], 1)
    for k in range(0, NB, GROUP):
        cols = [
            jnp.broadcast_to(work[:, k + i : k + i + 1], (NB, 2 * NB))
            for i in range(GROUP)
        ]
        lines = [work[k + i : k + i + 1, :] for i in range(GROUP)]
        piv = [[cols[j][k + i : k + i + 1, :] for j in range(GROUP)] for i in range(GROUP)]
        for i in range(GROUP):
            inv = 1.0 / piv[i][i]
            scaled = lines[i] * inv
            below = jnp.where(rows > k + i, cols[i], 0.0)
            work = work - below * scaled
            for j in range(i + 1, GROUP):
                f = piv[j][i] * inv
                lines[j] = lines[j] - f * lines[i]
                g = piv[i][j] * inv
                cols[j] = cols[j] - below * g
                for m in range(i + 1, GROUP):
                    piv[j][m] = piv[j][m] - f * piv[i][m]
    diag = jnp.sum(jnp.where(rows == lanes, work, 0.0), axis=1, keepdims=True)
    work = work * lax.rsqrt(diag)
    keep = (lanes >= rows) & ((lanes < NB) | (lanes <= rows + NB))
    return jnp.where(keep, work, 0.0)


def factor_kernel(gram_ref, upper_ref, inverse_ref, a_ref):
    order = gram_ref.shape[0]
    a_ref[...] = gram_ref[...]
    upper_ref[...] = jnp.zeros_like(upper_ref)
    r = lax.broadcasted_iota(jnp.int32, (order, order), 0)
    c = lax.broadcasted_iota(jnp.int32, (order, order), 1)
    inverse_ref[...] = (r == c).astype(jnp.float32)
    for lo in range(0, order, NB):
        hi = lo + NB
        done = eliminate(a_ref[lo:hi, lo:hi])
        inv = done[:, NB:]
        upper_ref[lo:hi, lo:hi] = done[:, :NB]
        new = dot32(inv, inverse_ref[lo:hi, :], ((1,), (0,)))
        inverse_ref[lo:hi, :] = new
        if hi < order:
            line = dot32(inv, a_ref[lo:hi, hi:], ((1,), (0,)))
            upper_ref[lo:hi, hi:] = line
            a_ref[hi:, hi:] = a_ref[hi:, hi:] - dot32(line, line, ((0,), (0,)))
            inverse_ref[hi:, :] = inverse_ref[hi:, :] - dot32(line, new, ((0,), (0,)))


def factor(gram):
    order = gram.shape[0]
    shape = jax.ShapeDtypeStruct((order, order), jnp.float32)
    return pl.pallas_call(
        factor_kernel,
        out_shape=(shape, shape),
        in_specs=[pl.BlockSpec(memory_space=pltpu.VMEM)],
        out_specs=(pl.BlockSpec(memory_space=pltpu.VMEM),) * 2,
        scratch_shapes=[pltpu.VMEM((order, order), jnp.float32)],
        compiler_params=pltpu.CompilerParams(vmem_limit_bytes=32 * 1024 * 1024),
        cost_estimate=pl.CostEstimate(
            flops=12 * order**3, bytes_accessed=12 * order**2, transcendentals=0
        ),
    )(gram)


TILE = 128


def level_plan(rows, levels):
    sizes = []
    size = rows
    for _ in range(levels):
        if size % 16 == 0:
            size //= 2
            sizes.append((size, True))
        else:
            sizes.append((size, False))
    return sizes


def sum_kernel(
    plans, orders, starts, landing, scale, width,
    gram_ref, term_ref, gram_out, term_out,
    part, inbox, full, send_sem, recv_sem,
):
    minor = lax.axis_size("grp")
    me = lax.axis_index("seg") * minor + lax.axis_index("grp")
    levels = len(orders[0])

    def bit_of(b):
        return (me // (1 << b)) % 2

    def device(b):
        other = me + (1 - 2 * bit_of(b)) * (1 << b)
        return (other // minor, other % minor)

    barrier = pltpu.get_barrier_semaphore()
    for b in range(levels):
        pl.semaphore_signal(
            barrier, inc=1, device_id=device(b), device_id_type=pl.DeviceIdType.MESH
        )

    blocks = width // TILE
    at = 0
    for i in range(blocks):
        for j in range(i, blocks):
            part[at : at + TILE, :] = (
                gram_ref[i * TILE : (i + 1) * TILE, j * TILE : (j + 1) * TILE] * scale
            )
            at += TILE
    for j in range(blocks):
        part[at : at + width, :] = term_ref[:, j * TILE : (j + 1) * TILE] * scale
        at += width
    pl.semaphore_wait(barrier, levels)

    streams = range(len(orders))
    offset = [[start] for start in starts]

    def aligned(value):
        return pl.multiple_of(value, 8)

    def scatter(s, level):
        size, halved = plans[s][level]
        b = orders[s][level]
        base = offset[s][-1]
        if halved:
            source = base + (1 - bit_of(b)) * size
            offset[s].append(base + bit_of(b) * size)
        else:
            source = base
            offset[s].append(base)
        copy = pltpu.make_async_remote_copy(
            src_ref=part.at[pl.ds(aligned(source), size)],
            dst_ref=inbox.at[pl.ds(landing[s][level], size)],
            send_sem=send_sem.at[s, level],
            recv_sem=recv_sem.at[s, level],
            device_id=device(b),
            device_id_type=pl.DeviceIdType.MESH,
        )
        copy.start()
        return copy

    flying = [scatter(s, 0) for s in streams]
    for level in range(levels):
        for s in streams:
            flying[s].wait()
            size = plans[s][level][0]
            here = pl.ds(aligned(offset[s][-1]), size)
            total = part[here, :] + inbox[landing[s][level] : landing[s][level] + size, :]
            if level + 1 < levels:
                part[here, :] = total
                flying[s] = scatter(s, level + 1)
            else:
                full[here, :] = total

    def gather(s, level):
        size, halved = plans[s][level]
        if not halved:
            return None
        here = pl.ds(aligned(offset[s][level + 1]), size)
        copy = pltpu.make_async_remote_copy(
            src_ref=full.at[here],
            dst_ref=full.at[here],
            send_sem=send_sem.at[s, levels + level],
            recv_sem=recv_sem.at[s, levels + level],
            device_id=device(orders[s][level]),
            device_id_type=pl.DeviceIdType.MESH,
        )
        copy.start()
        return copy

    flying = [gather(s, levels - 1) for s in streams]
    for level in range(levels - 1, -1, -1):
        for s in streams:
            if flying[s] is not None:
                flying[s].wait()
            if level > 0:
                flying[s] = gather(s, level - 1)

    at = 0
    for i in range(blocks):
        for j in range(blocks):
            here = (slice(i * TILE, (i + 1) * TILE), slice(j * TILE, (j + 1) * TILE))
            if j < i:
                gram_out[here] = jnp.zeros((TILE, TILE), jnp.float32)
            else:
                gram_out[here] = full[at : at + TILE, :]
                at += TILE
    for j in range(blocks):
        term_out[:, j * TILE : (j + 1) * TILE] = full[at : at + width, :]
        at += width


def summed(gram, term, scale):
    width = gram.shape[0]
    levels = lax.axis_size(AXES).bit_length() - 1
    blocks = width // TILE
    packed = blocks * (blocks + 1) // 2 * TILE
    half = blocks * width // 2
    lengths = (packed, half, half)
    starts = (0, packed, packed + half)
    rest = list(range(1, levels))
    orders = [[0] + rest[s:] + rest[:s] for s in range(3)]
    plans = [level_plan(length, levels) for length in lengths]
    landing = []
    at = 0
    for plan in plans:
        places = []
        for size, _ in plan:
            places.append(at)
            at += size
        landing.append(places)
    shape = jax.ShapeDtypeStruct((width, width), jnp.float32)
    rows = sum(lengths)
    return pl.pallas_call(
        functools.partial(
            sum_kernel, plans, orders, starts, landing, scale, width
        ),
        out_shape=(shape, shape),
        in_specs=[pl.BlockSpec(memory_space=pltpu.VMEM)] * 2,
        out_specs=(pl.BlockSpec(memory_space=pltpu.VMEM),) * 2,
        scratch_shapes=[
            pltpu.VMEM((rows, TILE), jnp.float32),
            pltpu.VMEM((at, TILE), jnp.float32),
            pltpu.VMEM((rows, TILE), jnp.float32),
            pltpu.SemaphoreType.DMA((3, 2 * levels)),
            pltpu.SemaphoreType.DMA((3, 2 * levels)),
        ],
        compiler_params=pltpu.CompilerParams(
            collective_id=0,
            has_side_effects=True,
            vmem_limit_bytes=32 * 1024 * 1024,
        ),
        cost_estimate=pl.CostEstimate(
            flops=rows * TILE, bytes_accessed=8 * rows * TILE, transcendentals=0
        ),
    )(gram, term)


def from_behind(block):
    count = lax.axis_size(AXES)
    route = [(i - 1, i) for i in range(1, count)]
    return lax.ppermute(block, AXES, route)


def shards(snapshots, upstream, velocity):
    high = lax.Precision.HIGH
    rows_here = snapshots.shape[0]
    count = rows_here * lax.axis_size(AXES)
    first_row = lax.axis_index(AXES) * rows_here
    arrived = from_behind(snapshots[rows_here - EDGE :])
    local_gram = jnp.dot(
        snapshots.T, snapshots, precision=high, preferred_element_type=jnp.float32
    )
    extended = jnp.concatenate([arrived, snapshots], 0)
    position = upstream - (first_row - EDGE)
    image = velocity[:, None] * (jnp.take(extended, position, axis=0) - snapshots)
    local_term = jnp.dot(
        snapshots.T, image, precision=high, preferred_element_type=jnp.float32
    )
    gram, term = summed(local_gram, local_term, 1.0 / count)
    upper, inverse = factor(gram)
    operator = dot32(dot32(inverse, term, ((1,), (0,))), inverse, ((1,), (1,)))
    return (operator, upper)


def solution(mesh):
    return jax.shard_map(
        shards,
        mesh=mesh,
        in_specs=(P(AXES, None), P(AXES), P(AXES)),
        out_specs=(P(), P()),
        check_vma=False,
    )
```

```python
import functools

import jax
import jax.numpy as jnp
from jax import lax
from jax.experimental import pallas as pl
from jax.experimental.pallas import tpu as pltpu
from jax.sharding import PartitionSpec as P

EDGE = 512
NB = 64
GROUP = 4
AXES = ("seg", "grp")


def dot32(a, b, dims):
    return lax.dot_general(
        a,
        b,
        (dims, ((), ())),
        precision=lax.Precision.HIGHEST,
        preferred_element_type=jnp.float32,
    )


def eliminate(block):
    rows = lax.broadcasted_iota(jnp.int32, (NB, 2 * NB), 0)
    lanes = lax.broadcasted_iota(jnp.int32, (NB, 2 * NB), 1)
    unit = (rows + NB == lanes).astype(jnp.float32)
    work = jnp.concatenate([block, unit[:, NB:]], 1)
    for k in range(0, NB, GROUP):
        cols = [
            jnp.broadcast_to(work[:, k + i : k + i + 1], (NB, 2 * NB))
            for i in range(GROUP)
        ]
        lines = [work[k + i : k + i + 1, :] for i in range(GROUP)]
        piv = [[cols[j][k + i : k + i + 1, :] for j in range(GROUP)] for i in range(GROUP)]
        for i in range(GROUP):
            inv = 1.0 / piv[i][i]
            scaled = lines[i] * inv
            below = jnp.where(rows > k + i, cols[i], 0.0)
            work = work - below * scaled
            for j in range(i + 1, GROUP):
                f = piv[j][i] * inv
                lines[j] = lines[j] - f * lines[i]
                g = piv[i][j] * inv
                cols[j] = cols[j] - below * g
                for m in range(i + 1, GROUP):
                    piv[j][m] = piv[j][m] - f * piv[i][m]
    diag = jnp.sum(jnp.where(rows == lanes, work, 0.0), axis=1, keepdims=True)
    work = work * lax.rsqrt(diag)
    keep = (lanes >= rows) & ((lanes < NB) | (lanes <= rows + NB))
    return jnp.where(keep, work, 0.0)


def factor_kernel(gram_ref, upper_ref, inverse_ref, a_ref):
    order = gram_ref.shape[0]
    a_ref[...] = gram_ref[...]
    upper_ref[...] = jnp.zeros_like(upper_ref)
    r = lax.broadcasted_iota(jnp.int32, (order, order), 0)
    c = lax.broadcasted_iota(jnp.int32, (order, order), 1)
    inverse_ref[...] = (r == c).astype(jnp.float32)
    for lo in range(0, order, NB):
        hi = lo + NB
        done = eliminate(a_ref[lo:hi, lo:hi])
        inv = done[:, NB:]
        upper_ref[lo:hi, lo:hi] = done[:, :NB]
        new = dot32(inv, inverse_ref[lo:hi, :], ((1,), (0,)))
        inverse_ref[lo:hi, :] = new
        if hi < order:
            line = dot32(inv, a_ref[lo:hi, hi:], ((1,), (0,)))
            upper_ref[lo:hi, hi:] = line
            a_ref[hi:, hi:] = a_ref[hi:, hi:] - dot32(line, line, ((0,), (0,)))
            inverse_ref[hi:, :] = inverse_ref[hi:, :] - dot32(line, new, ((0,), (0,)))


def factor(gram):
    order = gram.shape[0]
    shape = jax.ShapeDtypeStruct((order, order), jnp.float32)
    return pl.pallas_call(
        factor_kernel,
        out_shape=(shape, shape),
        in_specs=[pl.BlockSpec(memory_space=pltpu.VMEM)],
        out_specs=(pl.BlockSpec(memory_space=pltpu.VMEM),) * 2,
        scratch_shapes=[pltpu.VMEM((order, order), jnp.float32)],
        compiler_params=pltpu.CompilerParams(vmem_limit_bytes=32 * 1024 * 1024),
        cost_estimate=pl.CostEstimate(
            flops=12 * order**3, bytes_accessed=12 * order**2, transcendentals=0
        ),
    )(gram)


TILE = 128


def level_plan(rows, levels):
    sizes = []
    size = rows
    for _ in range(levels):
        if size % 16 == 0:
            size //= 2
            sizes.append((size, True))
        else:
            sizes.append((size, False))
    return sizes


def halves(value):
    top = value.astype(jnp.bfloat16)
    return top, (value - top.astype(jnp.float32)).astype(jnp.bfloat16)


def product(a, b, dims):
    return lax.dot_general(a, b, (dims, ((), ())), preferred_element_type=jnp.float32)


def column(ref, lo, hi, lanes):
    spread = jnp.broadcast_to(ref[:, lo:hi], (TILE, hi - lo)).T
    return jnp.concatenate([spread] * (lanes // TILE), 1)


def sum_kernel(
    plans, orders, starts, landing, scale, width,
    snap_ref, up_ref, vel_ref, gram_out, term_out,
    top, low, halo, part, inbox, full, send_sem, recv_sem, halo_sem,
):
    minor = lax.axis_size("grp")
    devices = lax.axis_size("seg") * minor
    me = lax.axis_index("seg") * minor + lax.axis_index("grp")
    levels = len(orders[0])
    rows = snap_ref.shape[0]

    def bit_of(b):
        return (me // (1 << b)) % 2

    def device(b):
        other = me + (1 - 2 * bit_of(b)) * (1 << b)
        return (other // minor, other % minor)

    ahead = (me + 1) % devices
    behind = (me + devices - 1) % devices
    barrier = pltpu.get_barrier_semaphore()
    for b in range(levels):
        pl.semaphore_signal(
            barrier, inc=1, device_id=device(b), device_id_type=pl.DeviceIdType.MESH
        )
    pl.semaphore_signal(
        barrier,
        inc=1,
        device_id=(behind // minor, behind % minor),
        device_id_type=pl.DeviceIdType.MESH,
    )
    for lo in range(0, rows, EDGE):
        t, l = halves(snap_ref[lo : lo + EDGE, :])
        top[lo : lo + EDGE, :] = t
        low[lo : lo + EDGE, :] = l
    both = ((0,), (0,))
    lead = product(top[...], top[...], both)
    cross = product(top[...], low[...], both)
    blocks = width // TILE
    at = 0
    for i in range(blocks):
        for j in range(i, blocks):
            si, sj = slice(i * TILE, (i + 1) * TILE), slice(j * TILE, (j + 1) * TILE)
            part[at : at + TILE, :] = (
                lead[si, sj] + (cross[si, sj] + cross[sj, si].T)
            ) * scale
            at += TILE
    pl.semaphore_wait(barrier, levels + 1)

    def aligned(value):
        return pl.multiple_of(value, 8)

    def stream(s):
        offset = [starts[s]]
        for level in range(levels):
            size, halved = plans[s][level]
            b = orders[s][level]
            base = offset[-1]
            source = base + (1 - bit_of(b)) * size if halved else base
            kept = base + bit_of(b) * size if halved else base
            offset.append(kept)
            land = landing[s][level]
            copy = pltpu.make_async_remote_copy(
                src_ref=part.at[pl.ds(aligned(source), size)],
                dst_ref=inbox.at[pl.ds(land, size)],
                send_sem=send_sem.at[s, level],
                recv_sem=recv_sem.at[s, level],
                device_id=device(b),
                device_id_type=pl.DeviceIdType.MESH,
            )
            copy.start()
            yield
            copy.wait()
            here = pl.ds(aligned(kept), size)
            total = part[here, :] + inbox[land : land + size, :]
            if level + 1 < levels:
                part[here, :] = total
            else:
                full[here, :] = total
        for level in range(levels - 1, -1, -1):
            size, halved = plans[s][level]
            if halved:
                here = pl.ds(aligned(offset[level + 1]), size)
                copy = pltpu.make_async_remote_copy(
                    src_ref=full.at[here],
                    dst_ref=full.at[here],
                    send_sem=send_sem.at[s, levels + level],
                    recv_sem=recv_sem.at[s, levels + level],
                    device_id=device(orders[s][level]),
                    device_id_type=pl.DeviceIdType.MESH,
                )
                copy.start()
                yield
                copy.wait()

    def advance(running):
        return [g for g in running if next(g, True) is None]

    halo_copy = pltpu.make_async_remote_copy(
        src_ref=snap_ref.at[pl.ds(rows - EDGE, EDGE)],
        dst_ref=halo,
        send_sem=halo_sem.at[0],
        recv_sem=halo_sem.at[1],
        device_id=(ahead // minor, ahead % minor),
        device_id_type=pl.DeviceIdType.MESH,
    )
    running = advance([stream(s) for s in range(3)])
    halo_copy.start()
    first_row = me * rows

    def share(lo, source_top, source_low, origin):
        hi = lo + EDGE
        span = source_top.shape[0]
        wanted = column(up_ref, lo, hi, TILE) - origin
        lane = lax.broadcasted_iota(jnp.int32, (EDGE, TILE), 1)
        pick = jnp.concatenate(
            [
                jnp.where(wanted == lane + c, 1.0, 0.0).astype(jnp.bfloat16)
                for c in range(0, span, TILE)
            ],
            1,
        )
        along = ((1,), (0,))
        feed = product(pick, source_top, along) + product(pick, source_low, along)
        image = column(vel_ref, lo, hi, width) * (feed - snap_ref[lo:hi, :])
        it, il = halves(image)
        return product(top[lo:hi, :], it, both) + (
            product(top[lo:hi, :], il, both) + product(low[lo:hi, :], it, both)
        )

    term = None
    for lo in range(EDGE, rows, EDGE):
        more = share(lo, top[: lo + EDGE, :], low[: lo + EDGE, :], first_row)
        term = more if term is None else term + more
        running = advance(running)
    halo_copy.wait()
    arrived = jnp.where(me > 0, halo[...], 0.0)
    ht, hl = halves(arrived)
    term = term + share(0, ht, hl, first_row - EDGE)
    at = starts[3]
    for j in range(blocks):
        part[at : at + width, :] = term[:, j * TILE : (j + 1) * TILE] * scale
        at += width
    running = running + advance([stream(s) for s in range(3, len(orders))])
    while running:
        running = advance(running)

    at = 0
    for i in range(blocks):
        for j in range(blocks):
            here = (slice(i * TILE, (i + 1) * TILE), slice(j * TILE, (j + 1) * TILE))
            if j < i:
                gram_out[here] = jnp.zeros((TILE, TILE), jnp.float32)
            else:
                gram_out[here] = full[at : at + TILE, :]
                at += TILE
    for j in range(blocks):
        term_out[:, j * TILE : (j + 1) * TILE] = full[at : at + width, :]
        at += width


def thirds(rows):
    unit = 256 if rows % 256 == 0 else 8
    units = rows // unit
    first = -(-units // 3)
    second = -(-(units - first) // 2)
    return [first * unit, second * unit, (units - first - second) * unit]


def summed(snapshots, upstream, velocity, scale):
    rows_here, width = snapshots.shape
    levels = lax.axis_size(AXES).bit_length() - 1
    blocks = width // TILE
    packed = blocks * (blocks + 1) // 2 * TILE
    lengths = thirds(packed) + thirds(blocks * width)
    starts = [sum(lengths[:s]) for s in range(len(lengths))]
    rest = list(range(1, levels))
    orders = [[0] + rest[s:] + rest[:s] for s in (0, 1, 2)] * 2
    plans = [level_plan(length, levels) for length in lengths]
    landing = []
    at = 0
    for plan in plans:
        places = []
        for size, _ in plan:
            places.append(at)
            at += size
        landing.append(places)
    shape = jax.ShapeDtypeStruct((width, width), jnp.float32)
    rows = sum(lengths)
    return pl.pallas_call(
        functools.partial(sum_kernel, plans, orders, starts, landing, scale, width),
        out_shape=(shape, shape),
        in_specs=[pl.BlockSpec(memory_space=pltpu.VMEM)] * 3,
        out_specs=(pl.BlockSpec(memory_space=pltpu.VMEM),) * 2,
        scratch_shapes=[
            pltpu.VMEM((rows_here, width), jnp.bfloat16),
            pltpu.VMEM((rows_here, width), jnp.bfloat16),
            pltpu.VMEM((EDGE, width), jnp.float32),
            pltpu.VMEM((rows, TILE), jnp.float32),
            pltpu.VMEM((at, TILE), jnp.float32),
            pltpu.VMEM((rows, TILE), jnp.float32),
            pltpu.SemaphoreType.DMA((len(lengths), 2 * levels)),
            pltpu.SemaphoreType.DMA((len(lengths), 2 * levels)),
            pltpu.SemaphoreType.DMA((2,)),
        ],
        compiler_params=pltpu.CompilerParams(
            collective_id=0,
            has_side_effects=True,
            vmem_limit_bytes=48 * 1024 * 1024,
        ),
        cost_estimate=pl.CostEstimate(
            flops=24 * rows_here * width**2,
            bytes_accessed=8 * rows * TILE,
            transcendentals=0,
        ),
    )(snapshots, upstream[None, :], velocity[None, :])


def shards(snapshots, upstream, velocity):
    count = snapshots.shape[0] * lax.axis_size(AXES)
    gram, term = summed(snapshots, upstream, velocity, 1.0 / count)
    upper, inverse = factor(gram)
    operator = dot32(dot32(inverse, term, ((1,), (0,))), inverse, ((1,), (1,)))
    return (operator, upper)


def solution(mesh):
    return jax.shard_map(
        shards,
        mesh=mesh,
        in_specs=(P(AXES, None), P(AXES), P(AXES)),
        out_specs=(P(), P()),
        check_vma=False,
    )
```

```python
import functools

import jax
import jax.numpy as jnp
from jax import lax
from jax.experimental import pallas as pl
from jax.experimental.pallas import tpu as pltpu
from jax.sharding import PartitionSpec as P

EDGE = 512
NB = 64
GROUP = 4
AXES = ("seg", "grp")


def dot32(a, b, dims):
    return lax.dot_general(
        a,
        b,
        (dims, ((), ())),
        precision=lax.Precision.HIGHEST,
        preferred_element_type=jnp.float32,
    )


def eliminate(block):
    rows = lax.broadcasted_iota(jnp.int32, (NB, 2 * NB), 0)
    lanes = lax.broadcasted_iota(jnp.int32, (NB, 2 * NB), 1)
    unit = (rows + NB == lanes).astype(jnp.float32)
    work = jnp.concatenate([block, unit[:, NB:]], 1)
    for k in range(0, NB, GROUP):
        cols = [
            jnp.broadcast_to(work[:, k + i : k + i + 1], (NB, 2 * NB))
            for i in range(GROUP)
        ]
        lines = [work[k + i : k + i + 1, :] for i in range(GROUP)]
        piv = [[cols[j][k + i : k + i + 1, :] for j in range(GROUP)] for i in range(GROUP)]
        for i in range(GROUP):
            inv = 1.0 / piv[i][i]
            scaled = lines[i] * inv
            below = jnp.where(rows > k + i, cols[i], 0.0)
            work = work - below * scaled
            for j in range(i + 1, GROUP):
                f = piv[j][i] * inv
                lines[j] = lines[j] - f * lines[i]
                g = piv[i][j] * inv
                cols[j] = cols[j] - below * g
                for m in range(i + 1, GROUP):
                    piv[j][m] = piv[j][m] - f * piv[i][m]
    diag = jnp.sum(jnp.where(rows == lanes, work, 0.0), axis=1, keepdims=True)
    work = work * lax.rsqrt(diag)
    keep = (lanes >= rows) & ((lanes < NB) | (lanes <= rows + NB))
    return jnp.where(keep, work, 0.0)


def factor(a_ref, upper_ref, inverse_ref, between):
    order = a_ref.shape[0]
    upper_ref[...] = jnp.zeros_like(upper_ref)
    r = lax.broadcasted_iota(jnp.int32, (order, order), 0)
    c = lax.broadcasted_iota(jnp.int32, (order, order), 1)
    inverse_ref[...] = (r == c).astype(jnp.float32)
    for lo in range(0, order, NB):
        hi = lo + NB
        done = eliminate(a_ref[lo:hi, lo:hi])
        between()
        inv = done[:, NB:]
        reach = -(-hi // TILE) * TILE
        new = dot32(inv, inverse_ref[lo:hi, :reach], ((1,), (0,)))
        if hi < order:
            start = hi // TILE * TILE
            line = dot32(inv, a_ref[lo:hi, start:], ((1,), (0,)))
            a_ref[start:, start:] = a_ref[start:, start:] - dot32(line, line, ((0,), (0,)))
            inverse_ref[start:, :reach] = inverse_ref[start:, :reach] - dot32(
                line, new, ((0,), (0,))
            )
            upper_ref[lo:hi, start:] = line
        upper_ref[lo:hi, lo:hi] = done[:, :NB]
        inverse_ref[lo:hi, :reach] = new
        between()


TILE = 128


def level_plan(rows, levels):
    sizes = []
    size = rows
    for _ in range(levels):
        if size % 16 == 0:
            size //= 2
            sizes.append((size, True))
        else:
            sizes.append((size, False))
    return sizes


def halves(value):
    top = value.astype(jnp.bfloat16)
    return top, (value - top.astype(jnp.float32)).astype(jnp.bfloat16)


def product(a, b, dims):
    return lax.dot_general(a, b, (dims, ((), ())), preferred_element_type=jnp.float32)


def column(ref, lo, hi, lanes):
    spread = jnp.broadcast_to(ref[:, lo:hi], (TILE, hi - lo)).T
    return jnp.concatenate([spread] * (lanes // TILE), 1)


def sum_kernel(
    plans, orders, starts, landing, scale, width,
    snap_ref, up_ref, vel_ref, operator_out, upper_out,
    gram, inverse, top, low, halo, part, inbox, full, send_sem, recv_sem, halo_sem,
):
    minor = lax.axis_size("grp")
    devices = lax.axis_size("seg") * minor
    me = lax.axis_index("seg") * minor + lax.axis_index("grp")
    levels = len(orders[0])
    rows = snap_ref.shape[0]

    def bit_of(b):
        return (me // (1 << b)) % 2

    def device(b):
        other = me + (1 - 2 * bit_of(b)) * (1 << b)
        return (other // minor, other % minor)

    ahead = (me + 1) % devices
    behind = (me + devices - 1) % devices
    barrier = pltpu.get_barrier_semaphore()
    for b in range(levels):
        pl.semaphore_signal(
            barrier, inc=1, device_id=device(b), device_id_type=pl.DeviceIdType.MESH
        )
    pl.semaphore_signal(
        barrier,
        inc=1,
        device_id=(behind // minor, behind % minor),
        device_id_type=pl.DeviceIdType.MESH,
    )
    for lo in range(0, rows, EDGE):
        t, l = halves(snap_ref[lo : lo + EDGE, :])
        top[lo : lo + EDGE, :] = t
        low[lo : lo + EDGE, :] = l
    both = ((0,), (0,))
    lead = product(top[...], top[...], both)
    cross = product(top[...], low[...], both)
    blocks = width // TILE
    at = 0
    for i in range(blocks):
        for j in range(i, blocks):
            si, sj = slice(i * TILE, (i + 1) * TILE), slice(j * TILE, (j + 1) * TILE)
            part[at : at + TILE, :] = (
                lead[si, sj] + (cross[si, sj] + cross[sj, si].T)
            ) * scale
            at += TILE
    pl.semaphore_wait(barrier, levels + 1)

    def aligned(value):
        return pl.multiple_of(value, 8)

    def stream(s):
        offset = [starts[s]]
        for level in range(levels):
            size, halved = plans[s][level]
            b = orders[s][level]
            base = offset[-1]
            source = base + (1 - bit_of(b)) * size if halved else base
            kept = base + bit_of(b) * size if halved else base
            offset.append(kept)
            land = landing[s][level]
            copy = pltpu.make_async_remote_copy(
                src_ref=part.at[pl.ds(aligned(source), size)],
                dst_ref=inbox.at[pl.ds(land, size)],
                send_sem=send_sem.at[s, level],
                recv_sem=recv_sem.at[s, level],
                device_id=device(b),
                device_id_type=pl.DeviceIdType.MESH,
            )
            copy.start()
            yield
            copy.wait()
            here = pl.ds(aligned(kept), size)
            total = part[here, :] + inbox[land : land + size, :]
            if level + 1 < levels:
                part[here, :] = total
            else:
                full[here, :] = total
        for level in range(levels - 1, -1, -1):
            size, halved = plans[s][level]
            if halved:
                here = pl.ds(aligned(offset[level + 1]), size)
                copy = pltpu.make_async_remote_copy(
                    src_ref=full.at[here],
                    dst_ref=full.at[here],
                    send_sem=send_sem.at[s, levels + level],
                    recv_sem=recv_sem.at[s, levels + level],
                    device_id=device(orders[s][level]),
                    device_id_type=pl.DeviceIdType.MESH,
                )
                copy.start()
                yield
                copy.wait()

    def advance(running):
        return [g for g in running if next(g, True) is None]

    halo_copy = pltpu.make_async_remote_copy(
        src_ref=snap_ref.at[pl.ds(rows - EDGE, EDGE)],
        dst_ref=halo,
        send_sem=halo_sem.at[0],
        recv_sem=halo_sem.at[1],
        device_id=(ahead // minor, ahead % minor),
        device_id_type=pl.DeviceIdType.MESH,
    )
    running = advance([stream(s) for s in range(3)])
    halo_copy.start()
    first_row = me * rows

    def share(lo, source_top, source_low, origin):
        hi = lo + EDGE
        span = source_top.shape[0]
        wanted = column(up_ref, lo, hi, TILE) - origin
        lane = lax.broadcasted_iota(jnp.int32, (EDGE, TILE), 1)
        pick = jnp.concatenate(
            [
                jnp.where(wanted == lane + c, 1.0, 0.0).astype(jnp.bfloat16)
                for c in range(0, span, TILE)
            ],
            1,
        )
        along = ((1,), (0,))
        feed = product(pick, source_top, along) + product(pick, source_low, along)
        image = column(vel_ref, lo, hi, width) * (feed - snap_ref[lo:hi, :])
        it, il = halves(image)
        return product(top[lo:hi, :], it, both) + (
            product(top[lo:hi, :], il, both) + product(low[lo:hi, :], it, both)
        )

    term = None
    for lo in range(EDGE, rows, EDGE):
        more = share(lo, top[: lo + EDGE, :], low[: lo + EDGE, :], first_row)
        term = more if term is None else term + more
        running = advance(running)
    halo_copy.wait()
    arrived = jnp.where(me > 0, halo[...], 0.0)
    ht, hl = halves(arrived)
    term = term + share(0, ht, hl, first_row - EDGE)
    at = starts[3]
    for j in range(blocks):
        part[at : at + width, :] = term[:, j * TILE : (j + 1) * TILE] * scale
        at += width
    later = advance([stream(s) for s in range(3, len(orders))])
    while running:
        running = advance(running)

    at = 0
    for i in range(blocks):
        for j in range(blocks):
            here = (slice(i * TILE, (i + 1) * TILE), slice(j * TILE, (j + 1) * TILE))
            if j < i:
                gram[here] = jnp.zeros((TILE, TILE), jnp.float32)
            else:
                gram[here] = full[at : at + TILE, :]
                at += TILE

    pending = [later]

    def between():
        pending[0] = advance(pending[0])

    factor(gram, upper_out, inverse, between)
    while pending[0]:
        between()
    for j in range(blocks):
        gram[:, j * TILE : (j + 1) * TILE] = full[at : at + width, :]
        at += width
    along = ((1,), (0,))
    left = dot32(inverse[...], gram[...], along)
    operator_out[...] = dot32(left, inverse[...], ((1,), (1,)))


def thirds(rows):
    unit = 256 if rows % 256 == 0 else 8
    units = rows // unit
    first = -(-units // 3)
    second = -(-(units - first) // 2)
    return [first * unit, second * unit, (units - first - second) * unit]


def projected(snapshots, upstream, velocity, scale):
    rows_here, width = snapshots.shape
    levels = lax.axis_size(AXES).bit_length() - 1
    blocks = width // TILE
    packed = blocks * (blocks + 1) // 2 * TILE
    lengths = thirds(packed) + thirds(blocks * width)
    starts = [sum(lengths[:s]) for s in range(len(lengths))]
    rest = list(range(1, levels))
    orders = [[0] + rest[s:] + rest[:s] for s in (0, 1, 2)] * 2
    plans = [level_plan(length, levels) for length in lengths]
    landing = []
    at = 0
    for plan in plans:
        places = []
        for size, _ in plan:
            places.append(at)
            at += size
        landing.append(places)
    shape = jax.ShapeDtypeStruct((width, width), jnp.float32)
    rows = sum(lengths)
    return pl.pallas_call(
        functools.partial(sum_kernel, plans, orders, starts, landing, scale, width),
        out_shape=(shape, shape),
        in_specs=[pl.BlockSpec(memory_space=pltpu.VMEM)] * 3,
        out_specs=(pl.BlockSpec(memory_space=pltpu.VMEM),) * 2,
        scratch_shapes=[
            pltpu.VMEM((width, width), jnp.float32),
            pltpu.VMEM((width, width), jnp.float32),
            pltpu.VMEM((rows_here, width), jnp.bfloat16),
            pltpu.VMEM((rows_here, width), jnp.bfloat16),
            pltpu.VMEM((EDGE, width), jnp.float32),
            pltpu.VMEM((rows, TILE), jnp.float32),
            pltpu.VMEM((at, TILE), jnp.float32),
            pltpu.VMEM((rows, TILE), jnp.float32),
            pltpu.SemaphoreType.DMA((len(lengths), 2 * levels)),
            pltpu.SemaphoreType.DMA((len(lengths), 2 * levels)),
            pltpu.SemaphoreType.DMA((2,)),
        ],
        compiler_params=pltpu.CompilerParams(
            collective_id=0,
            has_side_effects=True,
            vmem_limit_bytes=48 * 1024 * 1024,
        ),
        cost_estimate=pl.CostEstimate(
            flops=24 * rows_here * width**2,
            bytes_accessed=8 * rows * TILE,
            transcendentals=0,
        ),
    )(snapshots, upstream[None, :], velocity[None, :])


def shards(snapshots, upstream, velocity):
    count = snapshots.shape[0] * lax.axis_size(AXES)
    return projected(snapshots, upstream, velocity, 1.0 / count)


def solution(mesh):
    return jax.shard_map(
        shards,
        mesh=mesh,
        in_specs=(P(AXES, None), P(AXES), P(AXES)),
        out_specs=(P(), P()),
        check_vma=False,
    )
```

```python
import functools

import jax
import jax.numpy as jnp
from jax import lax
from jax.experimental import pallas as pl
from jax.experimental.pallas import tpu as pltpu
from jax.sharding import PartitionSpec as P

EDGE = 512
NB = 64
GROUP = 4
TILE = 128
AXES = ("seg", "grp")


def dot32(a, b, dims):
    return lax.dot_general(
        a,
        b,
        (dims, ((), ())),
        precision=lax.Precision.HIGHEST,
        preferred_element_type=jnp.float32,
    )


def eliminate(block):
    rows = lax.broadcasted_iota(jnp.int32, (NB, 2 * NB), 0)
    lanes = lax.broadcasted_iota(jnp.int32, (NB, 2 * NB), 1)
    unit = (rows + NB == lanes).astype(jnp.float32)
    work = jnp.concatenate([block, unit[:, NB:]], 1)
    for k in range(0, NB, GROUP):
        cols = [
            jnp.broadcast_to(work[:, k + i : k + i + 1], (NB, 2 * NB))
            for i in range(GROUP)
        ]
        lines = [work[k + i : k + i + 1, :] for i in range(GROUP)]
        piv = [[cols[j][k + i : k + i + 1, :] for j in range(GROUP)] for i in range(GROUP)]
        for i in range(GROUP):
            inv = 1.0 / piv[i][i]
            scaled = lines[i] * inv
            below = jnp.where(rows > k + i, cols[i], 0.0)
            work = work - below * scaled
            for j in range(i + 1, GROUP):
                f = piv[j][i] * inv
                lines[j] = lines[j] - f * lines[i]
                g = piv[i][j] * inv
                cols[j] = cols[j] - below * g
                for m in range(i + 1, GROUP):
                    piv[j][m] = piv[j][m] - f * piv[i][m]
    diag = jnp.sum(jnp.where(rows == lanes, work, 0.0), axis=1, keepdims=True)
    work = work * lax.rsqrt(diag)
    keep = (lanes >= rows) & ((lanes < NB) | (lanes <= rows + NB))
    return jnp.where(keep, work, 0.0)


def factor_kernel(gram_ref, upper_ref, inverse_ref, a_ref):
    order = gram_ref.shape[0]
    a_ref[...] = gram_ref[...]
    upper_ref[...] = jnp.zeros_like(upper_ref)
    r = lax.broadcasted_iota(jnp.int32, (order, order), 0)
    c = lax.broadcasted_iota(jnp.int32, (order, order), 1)
    inverse_ref[...] = (r == c).astype(jnp.float32)
    for lo in range(0, order, NB):
        hi = lo + NB
        done = eliminate(a_ref[lo:hi, lo:hi])
        inv = done[:, NB:]
        reach = -(-hi // TILE) * TILE
        new = dot32(inv, inverse_ref[lo:hi, :reach], ((1,), (0,)))
        if hi < order:
            start = hi // TILE * TILE
            line = dot32(inv, a_ref[lo:hi, start:], ((1,), (0,)))
            a_ref[start:, start:] = a_ref[start:, start:] - dot32(line, line, ((0,), (0,)))
            inverse_ref[start:, :reach] = inverse_ref[start:, :reach] - dot32(
                line, new, ((0,), (0,))
            )
            upper_ref[lo:hi, start:] = line
        upper_ref[lo:hi, lo:hi] = done[:, :NB]
        inverse_ref[lo:hi, :reach] = new


def factor(gram):
    order = gram.shape[0]
    shape = jax.ShapeDtypeStruct((order, order), jnp.float32)
    return pl.pallas_call(
        factor_kernel,
        out_shape=(shape, shape),
        in_specs=[pl.BlockSpec(memory_space=pltpu.VMEM)],
        out_specs=(pl.BlockSpec(memory_space=pltpu.VMEM),) * 2,
        scratch_shapes=[pltpu.VMEM((order, order), jnp.float32)],
        compiler_params=pltpu.CompilerParams(vmem_limit_bytes=32 * 1024 * 1024),
        cost_estimate=pl.CostEstimate(
            flops=12 * order**3, bytes_accessed=12 * order**2, transcendentals=0
        ),
    )(gram)


def level_plan(rows, levels):
    sizes = []
    size = rows
    for _ in range(levels):
        if size % 16 == 0:
            size //= 2
            sizes.append((size, True))
        else:
            sizes.append((size, False))
    return sizes


def halves(value):
    top = value.astype(jnp.bfloat16)
    return top, (value - top.astype(jnp.float32)).astype(jnp.bfloat16)


def product(a, b, dims):
    return lax.dot_general(a, b, (dims, ((), ())), preferred_element_type=jnp.float32)


def column(ref, lo, hi, lanes):
    spread = jnp.broadcast_to(ref[:, lo:hi], (TILE, hi - lo)).T
    return jnp.concatenate([spread] * (lanes // TILE), 1)


def sum_kernel(
    plans, orders, starts, landing, scale, width,
    snap_ref, up_ref, vel_ref, gram_out, term_out,
    top, low, halo, part, inbox, full, send_sem, recv_sem, halo_sem,
):
    minor = lax.axis_size("grp")
    devices = lax.axis_size("seg") * minor
    me = lax.axis_index("seg") * minor + lax.axis_index("grp")
    levels = len(orders[0])
    rows = snap_ref.shape[0]

    def bit_of(b):
        return (me // (1 << b)) % 2

    def device(b):
        other = me + (1 - 2 * bit_of(b)) * (1 << b)
        return (other // minor, other % minor)

    ahead = (me + 1) % devices
    behind = (me + devices - 1) % devices
    barrier = pltpu.get_barrier_semaphore()
    for b in range(levels):
        pl.semaphore_signal(
            barrier, inc=1, device_id=device(b), device_id_type=pl.DeviceIdType.MESH
        )
    pl.semaphore_signal(
        barrier,
        inc=1,
        device_id=(behind // minor, behind % minor),
        device_id_type=pl.DeviceIdType.MESH,
    )
    for lo in range(0, rows, EDGE):
        t, l = halves(snap_ref[lo : lo + EDGE, :])
        top[lo : lo + EDGE, :] = t
        low[lo : lo + EDGE, :] = l
    both = ((0,), (0,))
    lead = product(top[...], top[...], both)
    cross = product(top[...], low[...], both)
    blocks = width // TILE
    at = 0
    for i in range(blocks):
        for j in range(i, blocks):
            si, sj = slice(i * TILE, (i + 1) * TILE), slice(j * TILE, (j + 1) * TILE)
            part[at : at + TILE, :] = (
                lead[si, sj] + (cross[si, sj] + cross[sj, si].T)
            ) * scale
            at += TILE
    pl.semaphore_wait(barrier, levels + 1)

    def aligned(value):
        return pl.multiple_of(value, 8)

    def stream(s):
        offset = [starts[s]]
        for level in range(levels):
            size, halved = plans[s][level]
            b = orders[s][level]
            base = offset[-1]
            source = base + (1 - bit_of(b)) * size if halved else base
            kept = base + bit_of(b) * size if halved else base
            offset.append(kept)
            land = landing[s][level]
            copy = pltpu.make_async_remote_copy(
                src_ref=part.at[pl.ds(aligned(source), size)],
                dst_ref=inbox.at[pl.ds(land, size)],
                send_sem=send_sem.at[s, level],
                recv_sem=recv_sem.at[s, level],
                device_id=device(b),
                device_id_type=pl.DeviceIdType.MESH,
            )
            copy.start()
            yield
            copy.wait()
            here = pl.ds(aligned(kept), size)
            total = part[here, :] + inbox[land : land + size, :]
            if level + 1 < levels:
                part[here, :] = total
            else:
                full[here, :] = total
        for level in range(levels - 1, -1, -1):
            size, halved = plans[s][level]
            if halved:
                here = pl.ds(aligned(offset[level + 1]), size)
                copy = pltpu.make_async_remote_copy(
                    src_ref=full.at[here],
                    dst_ref=full.at[here],
                    send_sem=send_sem.at[s, levels + level],
                    recv_sem=recv_sem.at[s, levels + level],
                    device_id=device(orders[s][level]),
                    device_id_type=pl.DeviceIdType.MESH,
                )
                copy.start()
                yield
                copy.wait()

    def advance(running):
        return [g for g in running if next(g, True) is None]

    halo_copy = pltpu.make_async_remote_copy(
        src_ref=snap_ref.at[pl.ds(rows - EDGE, EDGE)],
        dst_ref=halo,
        send_sem=halo_sem.at[0],
        recv_sem=halo_sem.at[1],
        device_id=(ahead // minor, ahead % minor),
        device_id_type=pl.DeviceIdType.MESH,
    )
    running = advance([stream(s) for s in range(3)])
    halo_copy.start()
    first_row = me * rows

    def share(lo, source_top, source_low, origin):
        hi = lo + EDGE
        span = source_top.shape[0]
        wanted = column(up_ref, lo, hi, TILE) - origin
        lane = lax.broadcasted_iota(jnp.int32, (EDGE, TILE), 1)
        pick = jnp.concatenate(
            [
                jnp.where(wanted == lane + c, 1.0, 0.0).astype(jnp.bfloat16)
                for c in range(0, span, TILE)
            ],
            1,
        )
        along = ((1,), (0,))
        feed = product(pick, source_top, along) + product(pick, source_low, along)
        image = column(vel_ref, lo, hi, width) * (feed - snap_ref[lo:hi, :])
        it, il = halves(image)
        return product(top[lo:hi, :], it, both) + (
            product(top[lo:hi, :], il, both) + product(low[lo:hi, :], it, both)
        )

    term = None
    for lo in range(EDGE, rows, EDGE):
        more = share(lo, top[: lo + EDGE, :], low[: lo + EDGE, :], first_row)
        term = more if term is None else term + more
        running = advance(running)
    halo_copy.wait()
    arrived = jnp.where(me > 0, halo[...], 0.0)
    ht, hl = halves(arrived)
    term = term + share(0, ht, hl, first_row - EDGE)
    at = starts[3]
    for j in range(blocks):
        part[at : at + width, :] = term[:, j * TILE : (j + 1) * TILE] * scale
        at += width
    running = running + advance([stream(s) for s in range(3, len(orders))])
    while running:
        running = advance(running)

    at = 0
    for i in range(blocks):
        for j in range(blocks):
            here = (slice(i * TILE, (i + 1) * TILE), slice(j * TILE, (j + 1) * TILE))
            if j < i:
                gram_out[here] = jnp.zeros((TILE, TILE), jnp.float32)
            else:
                gram_out[here] = full[at : at + TILE, :]
                at += TILE
    for j in range(blocks):
        term_out[:, j * TILE : (j + 1) * TILE] = full[at : at + width, :]
        at += width


def thirds(rows):
    unit = 256 if rows % 256 == 0 else 8
    units = rows // unit
    first = -(-units // 3)
    second = -(-(units - first) // 2)
    return [first * unit, second * unit, (units - first - second) * unit]


def summed(snapshots, upstream, velocity, scale):
    rows_here, width = snapshots.shape
    levels = lax.axis_size(AXES).bit_length() - 1
    blocks = width // TILE
    packed = blocks * (blocks + 1) // 2 * TILE
    lengths = thirds(packed) + thirds(blocks * width)
    starts = [sum(lengths[:s]) for s in range(len(lengths))]
    rest = list(range(1, levels))
    orders = [[0] + rest[s:] + rest[:s] for s in (0, 1, 2)] * 2
    plans = [level_plan(length, levels) for length in lengths]
    landing = []
    at = 0
    for plan in plans:
        places = []
        for size, _ in plan:
            places.append(at)
            at += size
        landing.append(places)
    shape = jax.ShapeDtypeStruct((width, width), jnp.float32)
    rows = sum(lengths)
    return pl.pallas_call(
        functools.partial(sum_kernel, plans, orders, starts, landing, scale, width),
        out_shape=(shape, shape),
        in_specs=[pl.BlockSpec(memory_space=pltpu.VMEM)] * 3,
        out_specs=(pl.BlockSpec(memory_space=pltpu.VMEM),) * 2,
        scratch_shapes=[
            pltpu.VMEM((rows_here, width), jnp.bfloat16),
            pltpu.VMEM((rows_here, width), jnp.bfloat16),
            pltpu.VMEM((EDGE, width), jnp.float32),
            pltpu.VMEM((rows, TILE), jnp.float32),
            pltpu.VMEM((at, TILE), jnp.float32),
            pltpu.VMEM((rows, TILE), jnp.float32),
            pltpu.SemaphoreType.DMA((len(lengths), 2 * levels)),
            pltpu.SemaphoreType.DMA((len(lengths), 2 * levels)),
            pltpu.SemaphoreType.DMA((2,)),
        ],
        compiler_params=pltpu.CompilerParams(
            collective_id=0,
            has_side_effects=True,
            vmem_limit_bytes=48 * 1024 * 1024,
        ),
        cost_estimate=pl.CostEstimate(
            flops=24 * rows_here * width**2,
            bytes_accessed=8 * rows * TILE,
            transcendentals=0,
        ),
    )(snapshots, upstream[None, :], velocity[None, :])


def shards(snapshots, upstream, velocity):
    count = snapshots.shape[0] * lax.axis_size(AXES)
    gram, term = summed(snapshots, upstream, velocity, 1.0 / count)
    upper, inverse = factor(gram)
    operator = dot32(dot32(inverse, term, ((1,), (0,))), inverse, ((1,), (1,)))
    return (operator, upper)


def solution(mesh):
    return jax.shard_map(
        shards,
        mesh=mesh,
        in_specs=(P(AXES, None), P(AXES), P(AXES)),
        out_specs=(P(), P()),
        check_vma=False,
    )
```
